32 devices in a mesh: cfg: 2 (over y), row: 8 (over z, x), col: 2 (over core).
Axes of the slice: x: 2, y: 2, z: 4, core: 2. Of those that a mesh axis runs over, the one named last changes fastest.
Arguments:
- root_inv: bfloat16 [5120, 2560], P(('cfg', 'row'), 'col'), parts along dimension 0, as said below
- child_off: bfloat16 [2560, 65536], P('col', ('cfg', 'row')), parts along dimension 1, may hold values from -0.15625 to 0.15625
- child_inv: bfloat16 [4096, 65536], P('col', ('cfg', 'row')), parts along dimension 1, as said below
- struct: int32 [16, 5], P('cfg'), parts along dimension 0, may hold values from 0 to 9, as said below
Outputs:
- cross_cov: float32 [2560, 65536], P('col', ('cfg', 'row')), parts along dimension 1
- root_var: float32 [5120], P(('cfg', 'col')), parts along dimension 0
- child_var: float32 [65536], P(('cfg', 'row')), parts along dimension 0
The draws below stay inside these ranges and needn't reach their ends.
There are 2 independent parts, one for each index of `cfg`. The reference program is written for one: setup_inputs(seed, part) draws one part's arguments, and reference() takes and returns one part's arrays. A program takes and returns all parts, laid end to end along the dimension named above; each array names one. Nothing has to cross between parts.
Inputs may be any that keep to these rules, and one draw needn't show every extreme that they name: `struct`: row c lists the 256-row tiles of the root in which supernode c's block of L has nonzeros, all distinct; rows 2q and 2q + 1 together list every tile once. `root_inv`: lower triangular. `child_inv`: each block of 4096 columns is lower triangular.
All inputs are finite; a program needn't handle non-finite values.
Results may differ from the reference program's by a relative error of at most 0.0027.
Values may be sent and summed in bfloat16 or wider, within the bound.
A program may use at most 256 MiB of HBM per device.

```python
import math
import jax
import jax.numpy as jnp
from jax import lax

W0 = 2560
W1 = 4096
TILE = 256
CH = 8
COLS = 32768


def lower_factor(key, rows, cols, period, row_spread, col_spread):
    subkeys = jax.random.split(key, 5)
    row_ids = jnp.arange(rows)[:, None]
    col_ids = (jnp.arange(cols) % period)[None, :]
    noise_draw = jax.random.normal(subkeys[0], (rows, cols), jnp.float32)
    diagonal = jax.random.uniform(subkeys[2], (rows, 1), jnp.float32, 1.0, 2.0)
    trend_up = jnp.exp(math.log(3.0) * (row_ids.astype(jnp.float32) / rows - 0.5))
    row_scale = trend_up * jnp.exp(jax.random.uniform(subkeys[3], (rows, 1), jnp.float32, -1.0, 1.0) * math.log(row_spread))
    col_scale = jnp.exp(jax.random.uniform(subkeys[4], (1, cols), jnp.float32, -1.0, 1.0) * math.log(col_spread))
    entries = jnp.where(row_ids > col_ids, noise_draw / math.sqrt(period), 0.0)
    entries = jnp.where(row_ids == col_ids, diagonal, entries)
    return row_scale * col_scale * entries


def draw_root_inv(key, part):
    key = jax.random.fold_in(key, 11)
    values = lower_factor(key, W0, W0, W0, 2.0, 3.2)
    return values.astype(jnp.bfloat16)


def draw_child_inv(key, part):
    key = jax.random.fold_in(key, 17)
    values = lower_factor(key, W1, CH * W1, W1, 2.0, 3.2)
    return values.astype(jnp.bfloat16)


def draw_struct(key, part):
    key = jax.random.fold_in(key, 23)
    tile_count = W0 // TILE
    subkeys = jax.random.split(key, CH // 2)
    orders = jax.vmap(lambda single: jax.random.permutation(single, tile_count))(subkeys)
    return orders.astype(jnp.int32).reshape(CH, tile_count // 2)


def shard_levels(rng, dims, cuts, smallest, largest):
    gain, own = 1.0, jax.random.fold_in(rng, 6)
    for axis_at, shards_of in cuts:
        steps = jnp.exp(jax.random.uniform(jax.random.fold_in(own, axis_at), (shards_of,), jnp.float32, smallest / len(cuts), largest / len(cuts)))
        gain = gain * jnp.repeat(steps, dims[axis_at] // shards_of).reshape([-1 if axis == axis_at else 1 for axis in range(len(dims))])
    return gain


def normal_values(stream_key, extent, deviation, reach, cuts=(), held_as=jnp.bfloat16):
    level = shard_levels(stream_key, extent, cuts, -0.22, 0.18) if cuts else 1.0
    drawn = jax.random.normal(stream_key, extent, jnp.float32) * deviation * level
    return jnp.minimum(jnp.maximum(drawn, -reach), reach).astype(held_as)


def setup_inputs(seed: int = 0, part: int = 0) -> dict:
    key_of = jax.random.split(jax.random.key(seed), 5)
    part_splits = jax.random.split(jax.random.fold_in(key_of[4], part), 5)
    root_inv = draw_root_inv(jax.random.fold_in(jax.random.fold_in(key_of[4], part), 71), part)
    child_off = normal_values(part_splits[1], (W0, COLS), (W0 // 2) ** -0.5, 0.15625, ((0, 2), (1, 8)))
    child_inv = draw_child_inv(jax.random.fold_in(jax.random.fold_in(key_of[4], part), 71), part)
    struct = draw_struct(jax.random.fold_in(jax.random.fold_in(key_of[4], part), 71), part)
    return dict(root_inv=root_inv, child_off=child_off, child_inv=child_inv, struct=struct)


def member_mask(struct, row_ids, col_ids):
    tile_ids = row_ids // TILE
    tile_hits = jnp.any(tile_ids[:, None, None] == struct[None, :, :], axis=2).astype(jnp.float32)
    owners = col_ids // W1
    groups = jnp.arange(struct.shape[0], dtype=jnp.int32)
    choose = (owners[None, :] == groups[:, None]).astype(jnp.float32)
    return jnp.dot(tile_hits, choose, precision=lax.Precision.HIGHEST, preferred_element_type=jnp.float32) > 0.5


def reference(root_inv, child_off, child_inv, struct):
    member = member_mask(struct, jnp.arange(W0, dtype=jnp.int32), jnp.arange(CH * W1, dtype=jnp.int32))
    masked_off = jnp.where(member, child_off, jnp.zeros_like(child_off))
    product = jnp.dot(root_inv, masked_off, preferred_element_type=jnp.float32).astype(jnp.bfloat16)
    raw_cross = jnp.dot(root_inv.T, product, preferred_element_type=jnp.float32)
    cross_cov = jnp.where(member, -raw_cross, jnp.zeros_like(raw_cross))
    root_var = jnp.sum(jnp.square(root_inv.astype(jnp.float32)), axis=0)
    child_var = jnp.sum(jnp.square(child_inv.astype(jnp.float32)), axis=0) - jnp.sum(masked_off.astype(jnp.float32) * cross_cov, axis=0)
    return cross_cov, root_var, child_var
```

```python
import functools

import jax
import jax.numpy as jnp
from jax import lax
from jax.experimental import pallas as pl
from jax.experimental.pallas import tpu as pltpu
from jax.sharding import PartitionSpec as P

W1 = 4096
TILE = 256


def member_mask(struct, row_ids, col_ids):
    tile_ids = row_ids // TILE
    tile_hits = jnp.any(tile_ids[:, None, None] == struct[None, :, :], axis=2).astype(jnp.float32)
    owners = col_ids // W1
    groups = jnp.arange(struct.shape[0], dtype=jnp.int32)
    choose = (owners[None, :] == groups[:, None]).astype(jnp.float32)
    return (
        jnp.dot(
            tile_hits, choose, precision=lax.Precision.HIGHEST, preferred_element_type=jnp.float32
        )
        > 0.5
    )


def contract_rows(own_cols, product_rows):
    return lax.dot_general(
        own_cols, product_rows, (((0,), (0,)), ((), ())), preferred_element_type=jnp.float32
    )


def plain_body(root_inv, child_off, child_inv, struct):
    half_cols = root_inv.shape[1]
    col_count = child_off.shape[1]
    half_start = lax.axis_index("col") * half_cols
    col_start = lax.axis_index("row") * col_count
    row_ids = half_start + jnp.arange(half_cols, dtype=jnp.int32)
    col_ids = col_start + jnp.arange(col_count, dtype=jnp.int32)
    member = member_mask(struct, row_ids, col_ids)
    masked_off = jnp.where(member, child_off, jnp.zeros_like(child_off))
    root_var = lax.psum(jnp.sum(jnp.square(root_inv.astype(jnp.float32)), axis=0), "row")
    empty = (jnp.zeros((half_cols, col_count), jnp.float32), jnp.zeros((half_cols,), jnp.float32))
    first_terms = jnp.dot(
        lax.all_gather(root_inv, "row", axis=0, tiled=True),
        masked_off,
        preferred_element_type=jnp.float32,
    )
    product = lax.psum(first_terms, "col").astype(jnp.bfloat16)
    totals = (contract_rows(lax.all_gather(root_inv, "row", axis=0, tiled=True), product), empty[1])
    cross_cov = jnp.where(member, -totals[0], jnp.zeros_like(totals[0]))
    local_terms = jnp.sum(jnp.square(child_inv.astype(jnp.float32)), axis=0) - jnp.sum(
        masked_off.astype(jnp.float32) * cross_cov, axis=0
    )
    child_var = lax.psum(local_terms, "col")
    return (cross_cov, root_var, child_var)


MESH = pl.DeviceIdType.MESH
CHUNK = 512
LAG = 1


def gather_kernel(
    inv_ref, off_ref, mask_ref, r_out, p_out, var_out,
    r_buf, r_low, x_own, x_low, p_buf, r_masked, low_masked,
    recv_sem, send_sem, low_sem, x_sem, x_recv, p_send, p_recv, p_local, r_local, own_sem,
):
    rows, half = inv_ref.shape
    cols = off_ref.shape[1]
    row = lax.axis_index("row")
    core = lax.axis_index("col")
    z, x = row // 2, row % 2
    other = {"row": row, "col": 1 - core}
    across = {"row": 2 * z + 1 - x}
    below = {"row": lax.rem(row + 6, 8)}
    above = {"row": lax.rem(row + 2, 8)}
    widths = [min(half, -(-(k + 1) * rows // TILE) * TILE) for k in range(4)]

    barrier = pltpu.get_barrier_semaphore()
    pl.semaphore_signal(barrier, inc=1, device_id=across, device_id_type=MESH)
    pl.semaphore_signal(barrier, inc=1, device_id={"col": 1 - core}, device_id_type=MESH)

    @pl.when(z > 0)
    def _():
        pl.semaphore_signal(barrier, inc=1, device_id=below, device_id_type=MESH)

    @pl.when(z < 3)
    def _():
        pl.semaphore_signal(barrier, inc=1, device_id=above, device_id_type=MESH)

    own_copy = pltpu.make_async_copy(inv_ref, r_buf.at[row], own_sem)
    own_copy.start()
    x_copy = pltpu.make_async_copy(off_ref, x_own, x_sem.at[0])
    x_copy.start()
    pl.semaphore_wait(barrier, 3 + ((z + 1) // 2) % 2)

    send_x = pltpu.make_async_remote_copy(
        src_ref=off_ref, dst_ref=x_low, send_sem=x_sem.at[1], recv_sem=x_recv,
        device_id={"col": 1 - core}, device_id_type=MESH,
    )

    def block_at(step):
        s, flip = step // 2, step % 2
        first, second = 1 + z % 2, 2 * (1 - z % 2) + z // 2
        third = 3 * (1 - z // 2)
        zb = z + ((s + 3) // 4) * (first - z) + (s // 2) * (second - first) + (s // 3) * (third - second)
        return zb, flip, 2 * zb + (x + flip) % 2

    def by_width(block, act):
        depth = block - 4 * core
        for k in range(4):
            @pl.when((depth == k) if k < 3 else (depth >= 3))
            def _(k=k):
                act(widths[k])

    def send(block, width, way, device):
        view = r_buf.at[block, :, pl.ds(0, width)]
        return pltpu.make_async_remote_copy(
            src_ref=view, dst_ref=view, send_sem=send_sem.at[block, way], recv_sem=recv_sem.at[block],
            device_id=device, device_id_type=MESH,
        )

    def send_low(block):
        return pltpu.make_async_remote_copy(
            src_ref=r_buf.at[block], dst_ref=r_low.at[block - 4],
            send_sem=send_sem.at[block, 3], recv_sem=low_sem.at[block - 4],
            device_id={"col": 1 - core}, device_id_type=MESH,
        )

    def keep(block, width):
        return pltpu.make_async_copy(
            r_buf.at[block, :, pl.ds(0, width)],
            r_out.at[pl.ds(block * rows, rows), pl.ds(0, width)],
            r_local.at[block],
        )

    def keep_p(block, slot):
        return pltpu.make_async_copy(
            p_buf.at[slot], p_out.at[pl.ds(block * rows, rows), :], p_local.at[slot]
        )

    def send_p(block, slot):
        return pltpu.make_async_remote_copy(
            src_ref=p_buf.at[slot], dst_ref=p_out.at[pl.ds(block * rows, rows), :],
            send_sem=p_send.at[slot], recv_sem=p_recv.at[slot],
            device_id={"col": 1 - core}, device_id_type=MESH,
        )

    def each_send(step, act):
        zb, flip, block = block_at(step)

        def routes(width):
            @pl.when((flip == 0) & (zb >= z) & (z > 0))
            def _():
                act(send(block, width, 0, below))

            @pl.when((flip == 0) & (zb <= z) & (z < 3))
            def _():
                act(send(block, width, 1, above))

            @pl.when(flip == 0)
            def _():
                act(send(block, width, 2, across))

        by_width(block, routes)

        @pl.when((core == 0) & (block >= 4))
        def _():
            act(send_low(block))

    def pass_on(step):
        zb, flip, block = block_at(step)

        @pl.when(step == 0)
        def _():
            own_copy.wait()

        @pl.when(step > 0)
        def _():
            by_width(block, lambda width: send(block, width, 0, across).wait_recv())

        each_send(step, lambda copy: copy.start())
        by_width(block, lambda width: keep(block, width).start())

    def multiply(step):
        zb, flip, block = block_at(step)
        depth = block - 4 * core

        def squares(width):
            values = r_buf[block, :, :width].astype(jnp.float32)
            var_out[:, :width] += jnp.sum(values * values, axis=0, keepdims=True)

        by_width(block, squares)
        for k in range(4):
            @pl.when(depth == k)
            def _(k=k):
                width = widths[k]
                r_masked[:, :width] = r_buf[block, :, :width] * mask_ref[0:1, :width].astype(jnp.bfloat16)

                @pl.when(core == 0)
                def _():
                    @pl.loop(0, cols // CHUNK)
                    def _(j):
                        at = pl.ds(pl.multiple_of(j * CHUNK, CHUNK), CHUNK)
                        p_buf[k, :, at] = jnp.dot(
                            r_masked[:, :width], x_own[:width, at], preferred_element_type=jnp.float32
                        ).astype(jnp.bfloat16)

                @pl.when(core == 1)
                def _():
                    send_low(4 + k).wait_recv()
                    low_masked[...] = r_low[k] * mask_ref[1:2, :].astype(jnp.bfloat16)

                    @pl.loop(0, cols // CHUNK)
                    def _(j):
                        at = pl.ds(pl.multiple_of(j * CHUNK, CHUNK), CHUNK)
                        p_buf[k, :, at] = (
                            jnp.dot(low_masked[...], x_low[:, at], preferred_element_type=jnp.float32)
                            + jnp.dot(r_masked[:, :width], x_own[:width, at], preferred_element_type=jnp.float32)
                        ).astype(jnp.bfloat16)

                    send_p(4 + k, k).start()

                keep_p(4 * core + k, k).start()

    @pl.when(core == 0)
    def _():
        send_x.start()

    var_out[...] = jnp.zeros_like(var_out)
    pass_on(0)
    x_copy.wait()

    @pl.when(core == 1)
    def _():
        send_x.wait_recv()

    def turn(step, carry):
        @pl.when(step < 8)
        def _():
            pass_on(step)

        multiply(step - LAG)
        return carry

    lax.fori_loop(1, LAG, lambda step, carry: (pass_on(step), carry)[1], 0)
    lax.fori_loop(LAG, 8 + LAG, turn, 0)

    def finish(step, carry):
        each_send(step, lambda copy: copy.wait_send())
        block = block_at(step)[2]
        by_width(block, lambda width: keep(block, width).wait())
        return carry

    lax.fori_loop(0, 8, finish, 0)
    for k in range(4):
        keep_p(4 * core + k, k).wait()

    @pl.when(core == 0)
    def _():
        send_x.wait_send()
        for k in range(4):
            send_p(4 + k, k).wait_recv()

    @pl.when(core == 1)
    def _():
        for k in range(4):
            send_p(4 + k, k).wait_send()


def gather_product(root_inv, child_off, masks):
    rows, half = root_inv.shape
    cols = child_off.shape[1]
    bf16 = jnp.bfloat16
    dma = pltpu.SemaphoreType.DMA
    return pl.pallas_call(
        gather_kernel,
        out_shape=(
            jax.ShapeDtypeStruct((8 * rows, half), bf16),
            jax.ShapeDtypeStruct((8 * rows, cols), bf16),
            jax.ShapeDtypeStruct((1, half), jnp.float32),
        ),
        in_specs=[
            pl.BlockSpec(memory_space=pl.ANY),
            pl.BlockSpec(memory_space=pl.ANY),
            pl.BlockSpec(memory_space=pltpu.VMEM),
        ],
        out_specs=(
            pl.BlockSpec(memory_space=pl.ANY),
            pl.BlockSpec(memory_space=pl.ANY),
            pl.BlockSpec(memory_space=pltpu.VMEM),
        ),
        scratch_shapes=[
            pltpu.VMEM((8, rows, half), bf16),
            pltpu.VMEM((4, rows, half), bf16),
            pltpu.VMEM((half, cols), bf16),
            pltpu.VMEM((half, cols), bf16),
            pltpu.VMEM((4, rows, cols), bf16),
            pltpu.VMEM((rows, half), bf16),
            pltpu.VMEM((rows, half), bf16),
            dma((8,)), dma((8, 4)), dma((4,)), dma((2,)), dma(()), dma((4,)), dma((4,)), dma((4,)), dma((8,)), dma(()),
        ],
        compiler_params=pltpu.CompilerParams(
            collective_id=0, has_side_effects=True, vmem_limit_bytes=58 * 1024 * 1024
        ),
        cost_estimate=pl.CostEstimate(flops=36 * rows * rows * cols, bytes_accessed=60 * 2**20, transcendentals=0),
        name="gather_product",
    )(root_inv, child_off, masks)


def cross_kernel(starts, flags_ref, r_ref, p_ref, off_ref, y_ref, var_ref):
    var_ref[...] = jnp.zeros_like(var_ref)
    total = p_ref.shape[0]
    for t in range(len(starts)):
        tile = slice(t * TILE, (t + 1) * TILE)
        for core in range(2):
            @pl.when((flags_ref[t] == 1) & (flags_ref[len(starts)] == core))
            def _(t=t, core=core, tile=tile):
                low = core * (total // 2) + starts[t]
                y = -lax.dot_general(
                    r_ref[low:, tile], p_ref[low:, :], (((0,), (0,)), ((), ())),
                    preferred_element_type=jnp.float32,
                )
                y_ref[tile, :] = y
                var_ref[...] += jnp.sum(off_ref[tile, :].astype(jnp.float32) * y, axis=0, keepdims=True)

        @pl.when(flags_ref[t] == 0)
        def _(tile=tile):
            y_ref[tile, :] = jnp.zeros((TILE, y_ref.shape[1]), jnp.float32)


def cross_terms(flags, root_rows, product, child_off, rows):
    total, half = root_rows.shape
    cols = product.shape[1]
    widths = [min(half, -(-(k + 1) * rows // TILE) * TILE) for k in range(4)]
    starts = [rows * next(k for k in range(4) if widths[k] > t * TILE) for t in range(half // TILE)]
    return pl.pallas_call(
        functools.partial(cross_kernel, starts),
        grid_spec=pltpu.PrefetchScalarGridSpec(
            num_scalar_prefetch=1,
            grid=(cols // CHUNK,),
            in_specs=[
                pl.BlockSpec((total, half), lambda j, flags: (0, 0)),
                pl.BlockSpec((total, CHUNK), lambda j, flags: (0, j)),
                pl.BlockSpec((half, CHUNK), lambda j, flags: (0, j)),
            ],
            out_specs=[
                pl.BlockSpec((half, CHUNK), lambda j, flags: (0, j)),
                pl.BlockSpec((1, CHUNK), lambda j, flags: (0, j)),
            ],
        ),
        out_shape=(
            jax.ShapeDtypeStruct((half, cols), jnp.float32),
            jax.ShapeDtypeStruct((1, cols), jnp.float32),
        ),
        compiler_params=pltpu.CompilerParams(vmem_limit_bytes=56 * 1024 * 1024),
        name="cross_terms",
    )(flags, root_rows, product, child_off)


def fused_body(root_inv, child_off, child_inv, struct):
    rows, half = root_inv.shape
    cols = child_off.shape[1]
    tiles = half // TILE
    core = lax.axis_index("col")
    listed = lax.dynamic_slice_in_dim(struct, lax.axis_index("row") * cols // W1, 1, axis=0)[0]
    hits = jnp.any(jnp.arange(2 * tiles, dtype=jnp.int32)[:, None] == listed[None, :], axis=1)
    own_hits = lax.dynamic_slice_in_dim(hits, core * tiles, tiles, axis=0)
    masks = jnp.repeat(jnp.stack([own_hits, hits[:tiles]]).astype(jnp.float32), TILE, axis=1)
    root_rows, product, root_var = gather_product(root_inv, child_off, masks)
    flags = jnp.concatenate([own_hits.astype(jnp.int32), core[None].astype(jnp.int32)])
    cross_cov, cross_var = cross_terms(flags, root_rows, product, child_off, rows)
    local_terms = jnp.sum(jnp.square(child_inv.astype(jnp.float32)), axis=0) - cross_var[0]
    return (cross_cov, root_var[0], lax.psum(local_terms, "col"))


def body(row_devices, col_devices, root_inv, child_off, child_inv, struct):
    rows, half = root_inv.shape
    cols = child_off.shape[1]
    fits = (
        row_devices == 8 and col_devices == 2 and half == 4 * rows and half % TILE == 0
        and rows % 32 == 0 and half <= 1280 and cols <= 4096 and W1 % cols == 0 and cols % CHUNK == 0
    )
    run = fused_body if fits else plain_body
    return run(root_inv, child_off, child_inv, struct)


def solution(mesh):
    placed = (
        P(("cfg", "row"), "col"),
        P("col", ("cfg", "row")),
        P("col", ("cfg", "row")),
        P("cfg", None),
    )
    return jax.shard_map(
        functools.partial(body, mesh.shape["row"], mesh.shape["col"]),
        mesh=mesh,
        in_specs=placed,
        out_specs=(P("col", ("cfg", "row")), P(("cfg", "col")), P(("cfg", "row"))),
        check_vma=False,
    )
```

```python
import functools

import jax
import jax.numpy as jnp
from jax import lax
from jax.experimental import pallas as pl
from jax.experimental.pallas import tpu as pltpu
from jax.sharding import PartitionSpec as P

W1 = 4096
TILE = 256


def member_mask(struct, row_ids, col_ids):
    tile_ids = row_ids // TILE
    tile_hits = jnp.any(tile_ids[:, None, None] == struct[None, :, :], axis=2).astype(jnp.float32)
    owners = col_ids // W1
    groups = jnp.arange(struct.shape[0], dtype=jnp.int32)
    choose = (owners[None, :] == groups[:, None]).astype(jnp.float32)
    return (
        jnp.dot(
            tile_hits, choose, precision=lax.Precision.HIGHEST, preferred_element_type=jnp.float32
        )
        > 0.5
    )


def contract_rows(own_cols, product_rows):
    return lax.dot_general(
        own_cols, product_rows, (((0,), (0,)), ((), ())), preferred_element_type=jnp.float32
    )


def plain_body(root_inv, child_off, child_inv, struct):
    half_cols = root_inv.shape[1]
    col_count = child_off.shape[1]
    half_start = lax.axis_index("col") * half_cols
    col_start = lax.axis_index("row") * col_count
    row_ids = half_start + jnp.arange(half_cols, dtype=jnp.int32)
    col_ids = col_start + jnp.arange(col_count, dtype=jnp.int32)
    member = member_mask(struct, row_ids, col_ids)
    masked_off = jnp.where(member, child_off, jnp.zeros_like(child_off))
    root_var = lax.psum(jnp.sum(jnp.square(root_inv.astype(jnp.float32)), axis=0), "row")
    empty = (jnp.zeros((half_cols, col_count), jnp.float32), jnp.zeros((half_cols,), jnp.float32))
    first_terms = jnp.dot(
        lax.all_gather(root_inv, "row", axis=0, tiled=True),
        masked_off,
        preferred_element_type=jnp.float32,
    )
    product = lax.psum(first_terms, "col").astype(jnp.bfloat16)
    totals = (contract_rows(lax.all_gather(root_inv, "row", axis=0, tiled=True), product), empty[1])
    cross_cov = jnp.where(member, -totals[0], jnp.zeros_like(totals[0]))
    local_terms = jnp.sum(jnp.square(child_inv.astype(jnp.float32)), axis=0) - jnp.sum(
        masked_off.astype(jnp.float32) * cross_cov, axis=0
    )
    child_var = lax.psum(local_terms, "col")
    return (cross_cov, root_var, child_var)


MESH = pl.DeviceIdType.MESH
CHUNK = 512
LAG = 1
PARTS = 4


def gather_kernel(
    inv_ref, off_ref, child_ref, mask_ref, r_out, p_out, var_out, child_out,
    r_buf, r_low, x_own, x_low, p_buf, r_masked, low_masked, child_buf, child_sum,
    recv_sem, send_sem, low_sem, x_sem, x_recv, p_send, p_recv, p_local, r_local, own_sem, child_sem,
):
    rows, half = inv_ref.shape
    cols = off_ref.shape[1]
    part = rows // PARTS
    span = cols // PARTS
    child_rows = child_buf.shape[1]
    row = lax.axis_index("row")
    core = lax.axis_index("col")
    z, x = row // 2, row % 2
    other = {"row": row, "col": 1 - core}
    across = {"row": 2 * z + 1 - x}
    below = {"row": lax.rem(row + 6, 8)}
    above = {"row": lax.rem(row + 2, 8)}
    widths = [min(half, -(-(k + 1) * rows // TILE) * TILE) for k in range(4)]

    barrier = pltpu.get_barrier_semaphore()
    pl.semaphore_signal(barrier, inc=1, device_id=across, device_id_type=MESH)
    pl.semaphore_signal(barrier, inc=1, device_id={"col": 1 - core}, device_id_type=MESH)

    @pl.when(z > 0)
    def _():
        pl.semaphore_signal(barrier, inc=1, device_id=below, device_id_type=MESH)

    @pl.when(z < 3)
    def _():
        pl.semaphore_signal(barrier, inc=1, device_id=above, device_id_type=MESH)

    own_copy = pltpu.make_async_copy(inv_ref, r_buf.at[row], own_sem)
    own_copy.start()
    x_copy = pltpu.make_async_copy(off_ref, x_own, x_sem.at[0])
    x_copy.start()
    pl.semaphore_wait(barrier, 3 + ((z + 1) // 2) % 2)

    send_x = pltpu.make_async_remote_copy(
        src_ref=off_ref, dst_ref=x_low, send_sem=x_sem.at[1], recv_sem=x_recv,
        device_id={"col": 1 - core}, device_id_type=MESH,
    )

    def block_at(step):
        s, flip = step // 2, step % 2
        first, second = 1 + z % 2, 2 * (1 - z % 2) + z // 2
        third = 3 * (1 - z // 2)
        zb = z + ((s + 3) // 4) * (first - z) + (s // 2) * (second - first) + (s // 3) * (third - second)
        return zb, flip, 2 * zb + (x + flip) % 2

    def by_width(block, act):
        depth = block - 4 * core
        for k in range(4):
            @pl.when((depth == k) if k < 3 else (depth >= 3))
            def _(k=k):
                act(widths[k])

    def send(block, piece, width, way, device):
        view = r_buf.at[block, pl.ds(piece * part, part), pl.ds(0, width)]
        return pltpu.make_async_remote_copy(
            src_ref=view, dst_ref=view, send_sem=send_sem.at[block * PARTS + piece, way],
            recv_sem=recv_sem.at[block * PARTS + piece], device_id=device, device_id_type=MESH,
        )

    def send_low(block, piece):
        at = pl.ds(piece * part, part)
        return pltpu.make_async_remote_copy(
            src_ref=r_buf.at[block, at], dst_ref=r_low.at[block - 4, at],
            send_sem=send_sem.at[block * PARTS + piece, 3], recv_sem=low_sem.at[(block - 4) * PARTS + piece],
            device_id={"col": 1 - core}, device_id_type=MESH,
        )

    def keep(block, width):
        return pltpu.make_async_copy(
            r_buf.at[block, :, pl.ds(0, width)],
            r_out.at[pl.ds(block * rows, rows), pl.ds(0, width)],
            r_local.at[block],
        )

    def p_views(block, slot, piece):
        at = pl.ds(piece * span, span)
        return p_buf.at[slot, :, at], p_out.at[pl.ds(block * rows, rows), at]

    def keep_p(block, slot, piece):
        here, there = p_views(block, slot, piece)
        return pltpu.make_async_copy(here, there, p_local.at[slot * PARTS + piece])

    def send_p(block, slot, piece):
        here, there = p_views(block, slot, piece)
        return pltpu.make_async_remote_copy(
            src_ref=here, dst_ref=there,
            send_sem=p_send.at[slot * PARTS + piece], recv_sem=p_recv.at[slot * PARTS + piece],
            device_id={"col": 1 - core}, device_id_type=MESH,
        )

    def child_copy(turn):
        return pltpu.make_async_copy(
            child_ref.at[pl.ds(turn * child_rows, child_rows), :], child_buf.at[turn % 2], child_sem.at[turn % 2]
        )

    def child_squares(turn):
        @pl.when(turn + 1 < 8 * PARTS)
        def _():
            child_copy(turn + 1).start()

        child_copy(turn).wait()
        for first in range(0, cols, CHUNK):
            at = slice(first, first + CHUNK)
            total = child_sum[:, at]
            for low in range(0, child_rows, 16):
                values = child_buf[turn % 2, low : low + 16, at].astype(jnp.float32)
                total += values[:8] * values[:8] + values[8:] * values[8:]
            child_sum[:, at] = total

    def each_send(step, piece, act):
        zb, flip, block = block_at(step)

        def routes(width):
            @pl.when((flip == 0) & (zb >= z) & (z > 0))
            def _():
                act(send(block, piece, width, 0, below))

            @pl.when((flip == 0) & (zb <= z) & (z < 3))
            def _():
                act(send(block, piece, width, 1, above))

            @pl.when(flip == 0)
            def _():
                act(send(block, piece, width, 2, across))

        by_width(block, routes)

        @pl.when((core == 0) & (block >= 4))
        def _():
            act(send_low(block, piece))

    def pass_on(step, piece):
        zb, flip, block = block_at(step)

        @pl.when((step == 0) & (piece == 0))
        def _():
            own_copy.wait()

        @pl.when(step > 0)
        def _():
            by_width(block, lambda width: send(block, piece, width, 0, across).wait_recv())

        each_send(step, piece, lambda copy: copy.start())

        @pl.when(piece == PARTS - 1)
        def _():
            by_width(block, lambda width: keep(block, width).start())

    def multiply(step, piece):
        zb, flip, block = block_at(step)
        depth = block - 4 * core

        def squares(width):
            values = r_buf[block, pl.ds(piece * part, part), :width].astype(jnp.float32)
            var_out[:, :width] += jnp.sum(values * values, axis=0, keepdims=True)

        by_width(block, squares)
        for k in range(4):
            @pl.when(depth == k)
            def _(k=k):
                width = widths[k]

                @pl.when(piece == 0)
                def _():
                    r_masked[:, :width] = r_buf[block, :, :width] * mask_ref[0:1, :width].astype(jnp.bfloat16)

                @pl.when((piece == 0) & (core == 1))
                def _():
                    for each in range(PARTS):
                        send_low(4 + k, each).wait_recv()
                    low_masked[...] = r_low[k] * mask_ref[1:2, :].astype(jnp.bfloat16)

                @pl.when(core == 0)
                def _():
                    @pl.loop(0, span // CHUNK)
                    def _(j):
                        at = pl.ds(pl.multiple_of(piece * span + j * CHUNK, CHUNK), CHUNK)
                        p_buf[k, :, at] = jnp.dot(
                            r_masked[:, :width], x_own[:width, at], preferred_element_type=jnp.float32
                        ).astype(jnp.bfloat16)

                @pl.when(core == 1)
                def _():
                    @pl.loop(0, span // CHUNK)
                    def _(j):
                        at = pl.ds(pl.multiple_of(piece * span + j * CHUNK, CHUNK), CHUNK)
                        p_buf[k, :, at] = (
                            jnp.dot(low_masked[...], x_low[:, at], preferred_element_type=jnp.float32)
                            + jnp.dot(r_masked[:, :width], x_own[:width, at], preferred_element_type=jnp.float32)
                        ).astype(jnp.bfloat16)

                    send_p(4 + k, k, piece).start()

                keep_p(4 * core + k, k, piece).start()

    child_copy(0).start()

    @pl.when(core == 0)
    def _():
        send_x.start()

    var_out[...] = jnp.zeros_like(var_out)
    child_sum[...] = jnp.zeros_like(child_sum)
    first_low = 2 * (2 - z) * (1 - z // 2)

    def turn(n, carry):
        step, piece = n // PARTS, n % PARTS

        @pl.when(n < 8 * PARTS)
        def _():
            pass_on(step, piece)
            child_squares(n)

        @pl.when(n == LAG * PARTS)
        def _():
            x_copy.wait()

        @pl.when((core == 1) & (n == (first_low + LAG) * PARTS))
        def _():
            send_x.wait_recv()

        @pl.when(n >= LAG * PARTS)
        def _():
            multiply(step - LAG, piece)

        return carry

    lax.fori_loop(0, (8 + LAG) * PARTS, turn, 0)
    child_out[...] = jnp.sum(child_sum[...], axis=0, keepdims=True)

    def finish(n, carry):
        each_send(n // PARTS, n % PARTS, lambda copy: copy.wait_send())
        return carry

    lax.fori_loop(0, 8 * PARTS, finish, 0)

    def kept(step, carry):
        block = block_at(step)[2]
        by_width(block, lambda width: keep(block, width).wait())
        return carry

    lax.fori_loop(0, 8, kept, 0)

    def product_done(n, carry):
        slot, piece = n // PARTS, n % PARTS
        keep_p(4 * core + slot, slot, piece).wait()

        @pl.when(core == 0)
        def _():
            send_p(4 + slot, slot, piece).wait_recv()

        @pl.when(core == 1)
        def _():
            send_p(4 + slot, slot, piece).wait_send()

        return carry

    lax.fori_loop(0, 4 * PARTS, product_done, 0)

    @pl.when(core == 0)
    def _():
        send_x.wait_send()


def gather_product(root_inv, child_off, child_inv, masks):
    rows, half = root_inv.shape
    cols = child_off.shape[1]
    bf16 = jnp.bfloat16
    dma = pltpu.SemaphoreType.DMA
    return pl.pallas_call(
        gather_kernel,
        out_shape=(
            jax.ShapeDtypeStruct((8 * rows, half), bf16),
            jax.ShapeDtypeStruct((8 * rows, cols), bf16),
            jax.ShapeDtypeStruct((1, half), jnp.float32),
            jax.ShapeDtypeStruct((1, cols), jnp.float32),
        ),
        in_specs=[
            pl.BlockSpec(memory_space=pl.ANY),
            pl.BlockSpec(memory_space=pl.ANY),
            pl.BlockSpec(memory_space=pl.ANY),
            pl.BlockSpec(memory_space=pltpu.VMEM),
        ],
        out_specs=(
            pl.BlockSpec(memory_space=pl.ANY),
            pl.BlockSpec(memory_space=pl.ANY),
            pl.BlockSpec(memory_space=pltpu.VMEM),
            pl.BlockSpec(memory_space=pltpu.VMEM),
        ),
        scratch_shapes=[
            pltpu.VMEM((8, rows, half), bf16),
            pltpu.VMEM((4, rows, half), bf16),
            pltpu.VMEM((half, cols), bf16),
            pltpu.VMEM((half, cols), bf16),
            pltpu.VMEM((4, rows, cols), bf16),
            pltpu.VMEM((rows, half), bf16),
            pltpu.VMEM((rows, half), bf16),
            pltpu.VMEM((2, child_inv.shape[0] // (8 * PARTS), cols), bf16),
            pltpu.VMEM((8, cols), jnp.float32),
            dma((8 * PARTS,)), dma((8 * PARTS, 4)), dma((4 * PARTS,)), dma((2,)), dma(()),
            dma((4 * PARTS,)), dma((4 * PARTS,)), dma((4 * PARTS,)), dma((8,)), dma(()), dma((2,)),
        ],
        compiler_params=pltpu.CompilerParams(
            collective_id=0, has_side_effects=True, vmem_limit_bytes=58 * 1024 * 1024
        ),
        cost_estimate=pl.CostEstimate(flops=36 * rows * rows * cols, bytes_accessed=60 * 2**20, transcendentals=0),
        name="gather_product",
    )(root_inv, child_off, child_inv, masks)


def cross_kernel(starts, flags_ref, r_ref, p_ref, off_ref, y_ref, var_ref):
    var_ref[...] = jnp.zeros_like(var_ref)
    total = p_ref.shape[0]
    for t in range(len(starts)):
        tile = slice(t * TILE, (t + 1) * TILE)
        for core in range(2):
            @pl.when((flags_ref[t] == 1) & (flags_ref[len(starts)] == core))
            def _(t=t, core=core, tile=tile):
                low = core * (total // 2) + starts[t]
                y = -lax.dot_general(
                    r_ref[low:, tile], p_ref[low:, :], (((0,), (0,)), ((), ())),
                    preferred_element_type=jnp.float32,
                )
                y_ref[tile, :] = y
                var_ref[...] += jnp.sum(off_ref[tile, :].astype(jnp.float32) * y, axis=0, keepdims=True)

        @pl.when(flags_ref[t] == 0)
        def _(tile=tile):
            y_ref[tile, :] = jnp.zeros((TILE, y_ref.shape[1]), jnp.float32)


def cross_terms(flags, root_rows, product, child_off, rows):
    total, half = root_rows.shape
    cols = product.shape[1]
    widths = [min(half, -(-(k + 1) * rows // TILE) * TILE) for k in range(4)]
    starts = [rows * next(k for k in range(4) if widths[k] > t * TILE) for t in range(half // TILE)]
    return pl.pallas_call(
        functools.partial(cross_kernel, starts),
        grid_spec=pltpu.PrefetchScalarGridSpec(
            num_scalar_prefetch=1,
            grid=(cols // CHUNK,),
            in_specs=[
                pl.BlockSpec((total, half), lambda j, flags: (0, 0)),
                pl.BlockSpec((total, CHUNK), lambda j, flags: (0, j)),
                pl.BlockSpec((half, CHUNK), lambda j, flags: (0, j)),
            ],
            out_specs=[
                pl.BlockSpec((half, CHUNK), lambda j, flags: (0, j)),
                pl.BlockSpec((1, CHUNK), lambda j, flags: (0, j)),
            ],
        ),
        out_shape=(
            jax.ShapeDtypeStruct((half, cols), jnp.float32),
            jax.ShapeDtypeStruct((1, cols), jnp.float32),
        ),
        compiler_params=pltpu.CompilerParams(vmem_limit_bytes=56 * 1024 * 1024),
        name="cross_terms",
    )(flags, root_rows, product, child_off)


def fused_body(root_inv, child_off, child_inv, struct):
    rows, half = root_inv.shape
    cols = child_off.shape[1]
    tiles = half // TILE
    core = lax.axis_index("col")
    listed = lax.dynamic_slice_in_dim(struct, lax.axis_index("row") * cols // W1, 1, axis=0)[0]
    hits = jnp.any(jnp.arange(2 * tiles, dtype=jnp.int32)[:, None] == listed[None, :], axis=1)
    own_hits = lax.dynamic_slice_in_dim(hits, core * tiles, tiles, axis=0)
    masks = jnp.repeat(jnp.stack([own_hits, hits[:tiles]]).astype(jnp.float32), TILE, axis=1)
    root_rows, product, root_var, child_squares = gather_product(root_inv, child_off, child_inv, masks)
    flags = jnp.concatenate([own_hits.astype(jnp.int32), core[None].astype(jnp.int32)])
    cross_cov, cross_var = cross_terms(flags, root_rows, product, child_off, rows)
    local_terms = child_squares[0] - cross_var[0]
    return (cross_cov, root_var[0], lax.psum(local_terms, "col"))


def body(row_devices, col_devices, root_inv, child_off, child_inv, struct):
    rows, half = root_inv.shape
    cols = child_off.shape[1]
    fits = (
        row_devices == 8 and col_devices == 2 and half == 4 * rows and half % TILE == 0
        and rows % 64 == 0 and child_inv.shape[0] % 512 == 0 and half <= 1280 and cols <= 4096 and W1 % cols == 0 and cols % (PARTS * CHUNK) == 0
    )
    run = fused_body if fits else plain_body
    return run(root_inv, child_off, child_inv, struct)


def solution(mesh):
    placed = (
        P(("cfg", "row"), "col"),
        P("col", ("cfg", "row")),
        P("col", ("cfg", "row")),
        P("cfg", None),
    )
    return jax.shard_map(
        functools.partial(body, mesh.shape["row"], mesh.shape["col"]),
        mesh=mesh,
        in_specs=placed,
        out_specs=(P("col", ("cfg", "row")), P(("cfg", "col")), P(("cfg", "row"))),
        check_vma=False,
    )
```

```python
import functools

import jax
import jax.numpy as jnp
from jax import lax
from jax.experimental import pallas as pl
from jax.experimental.pallas import tpu as pltpu
from jax.sharding import PartitionSpec as P

W1 = 4096
TILE = 256


def member_mask(struct, row_ids, col_ids):
    tile_ids = row_ids // TILE
    tile_hits = jnp.any(tile_ids[:, None, None] == struct[None, :, :], axis=2).astype(jnp.float32)
    owners = col_ids // W1
    groups = jnp.arange(struct.shape[0], dtype=jnp.int32)
    choose = (owners[None, :] == groups[:, None]).astype(jnp.float32)
    return (
        jnp.dot(
            tile_hits, choose, precision=lax.Precision.HIGHEST, preferred_element_type=jnp.float32
        )
        > 0.5
    )


def contract_rows(own_cols, product_rows):
    return lax.dot_general(
        own_cols, product_rows, (((0,), (0,)), ((), ())), preferred_element_type=jnp.float32
    )


def plain_body(root_inv, child_off, child_inv, struct):
    half_cols = root_inv.shape[1]
    col_count = child_off.shape[1]
    half_start = lax.axis_index("col") * half_cols
    col_start = lax.axis_index("row") * col_count
    row_ids = half_start + jnp.arange(half_cols, dtype=jnp.int32)
    col_ids = col_start + jnp.arange(col_count, dtype=jnp.int32)
    member = member_mask(struct, row_ids, col_ids)
    masked_off = jnp.where(member, child_off, jnp.zeros_like(child_off))
    root_var = lax.psum(jnp.sum(jnp.square(root_inv.astype(jnp.float32)), axis=0), "row")
    empty = (jnp.zeros((half_cols, col_count), jnp.float32), jnp.zeros((half_cols,), jnp.float32))
    first_terms = jnp.dot(
        lax.all_gather(root_inv, "row", axis=0, tiled=True),
        masked_off,
        preferred_element_type=jnp.float32,
    )
    product = lax.psum(first_terms, "col").astype(jnp.bfloat16)
    totals = (contract_rows(lax.all_gather(root_inv, "row", axis=0, tiled=True), product), empty[1])
    cross_cov = jnp.where(member, -totals[0], jnp.zeros_like(totals[0]))
    local_terms = jnp.sum(jnp.square(child_inv.astype(jnp.float32)), axis=0) - jnp.sum(
        masked_off.astype(jnp.float32) * cross_cov, axis=0
    )
    child_var = lax.psum(local_terms, "col")
    return (cross_cov, root_var, child_var)


MESH = pl.DeviceIdType.MESH
CHUNK = 512
PARTS = 4
LAG = 3
BLOCK = 1024


def gather_kernel(
    inv_ref, off_ref, child_ref, mask_ref, r_out, p_out, var_out, child_out,
    r_buf, r_low, x_own, x_low, p_buf, r_masked, low_masked, child_buf, child_sum,
    recv_sem, send_sem, low_sem, x_sem, x_recv, p_send, p_recv, p_local, r_local, own_sem, child_sem,
):
    rows, half = inv_ref.shape
    cols = off_ref.shape[1]
    part = rows // PARTS
    span = cols // PARTS
    child_rows = child_buf.shape[1]
    row = lax.axis_index("row")
    core = lax.axis_index("col")
    z, x = row // 2, row % 2
    other = {"row": row, "col": 1 - core}
    across = {"row": 2 * z + 1 - x}
    below = {"row": lax.rem(row + 6, 8)}
    above = {"row": lax.rem(row + 2, 8)}
    widths = [min(half, -(-(k + 1) * rows // TILE) * TILE) for k in range(4)]

    barrier = pltpu.get_barrier_semaphore()
    pl.semaphore_signal(barrier, inc=1, device_id=across, device_id_type=MESH)
    pl.semaphore_signal(barrier, inc=1, device_id={"col": 1 - core}, device_id_type=MESH)

    @pl.when(z > 0)
    def _():
        pl.semaphore_signal(barrier, inc=1, device_id=below, device_id_type=MESH)

    @pl.when(z < 3)
    def _():
        pl.semaphore_signal(barrier, inc=1, device_id=above, device_id_type=MESH)

    own_copy = pltpu.make_async_copy(inv_ref, r_buf.at[row], own_sem)
    own_copy.start()
    x_copy = pltpu.make_async_copy(off_ref, x_own, x_sem.at[0])
    x_copy.start()
    pl.semaphore_wait(barrier, 3 + ((z + 1) // 2) % 2)

    send_x = pltpu.make_async_remote_copy(
        src_ref=off_ref, dst_ref=x_low, send_sem=x_sem.at[1], recv_sem=x_recv,
        device_id={"col": 1 - core}, device_id_type=MESH,
    )

    def block_at(step):
        s, flip = step // 2, step % 2
        first, second = 1 + z % 2, 2 * (1 - z % 2) + z // 2
        third = 3 * (1 - z // 2)
        zb = z + ((s + 3) // 4) * (first - z) + (s // 2) * (second - first) + (s // 3) * (third - second)
        return zb, flip, 2 * zb + (x + flip) % 2

    def by_width(block, act):
        depth = block - 4 * core
        for k in range(4):
            @pl.when((depth == k) if k < 3 else (depth >= 3))
            def _(k=k):
                act(widths[k])

    def send(block, piece, width, way, device):
        view = r_buf.at[block, pl.ds(piece * part, part), pl.ds(0, width)]
        return pltpu.make_async_remote_copy(
            src_ref=view, dst_ref=view, send_sem=send_sem.at[block * PARTS + piece, way],
            recv_sem=recv_sem.at[block * PARTS + piece], device_id=device, device_id_type=MESH,
        )

    def send_low(block, piece):
        at = pl.ds(piece * part, part)
        return pltpu.make_async_remote_copy(
            src_ref=r_buf.at[block, at], dst_ref=r_low.at[block - 4, at],
            send_sem=send_sem.at[block * PARTS + piece, 3], recv_sem=low_sem.at[(block - 4) * PARTS + piece],
            device_id={"col": 1 - core}, device_id_type=MESH,
        )

    def keep(block, width):
        return pltpu.make_async_copy(
            r_buf.at[block, :, pl.ds(0, width)],
            r_out.at[pl.ds(block * rows, rows), pl.ds(0, width)],
            r_local.at[block],
        )

    def p_views(block, slot, piece):
        at = pl.ds(piece * span, span)
        return p_buf.at[slot, :, at], p_out.at[pl.ds(block * rows, rows), at]

    def keep_p(block, slot, piece):
        here, there = p_views(block, slot, piece)
        return pltpu.make_async_copy(here, there, p_local.at[slot * PARTS + piece])

    def send_p(block, slot, piece):
        here, there = p_views(block, slot, piece)
        return pltpu.make_async_remote_copy(
            src_ref=here, dst_ref=there,
            send_sem=p_send.at[slot * PARTS + piece], recv_sem=p_recv.at[slot * PARTS + piece],
            device_id={"col": 1 - core}, device_id_type=MESH,
        )

    def child_copy(turn):
        return pltpu.make_async_copy(
            child_ref.at[pl.ds(turn * child_rows, child_rows), :], child_buf.at[turn % 2], child_sem.at[turn % 2]
        )

    def child_squares(turn):
        @pl.when(turn + 1 < 8 * PARTS)
        def _():
            child_copy(turn + 1).start()

        child_copy(turn).wait()
        for first in range(0, cols, CHUNK):
            at = slice(first, first + CHUNK)
            total = child_sum[:, at]
            for low in range(0, child_rows, 16):
                values = child_buf[turn % 2, low : low + 16, at].astype(jnp.float32)
                total += values[:8] * values[:8] + values[8:] * values[8:]
            child_sum[:, at] = total

    def each_send(step, piece, act):
        zb, flip, block = block_at(step)

        def routes(width):
            @pl.when((flip == 0) & (zb >= z) & (z > 0))
            def _():
                act(send(block, piece, width, 0, below))

            @pl.when((flip == 0) & (zb <= z) & (z < 3))
            def _():
                act(send(block, piece, width, 1, above))

            @pl.when(flip == 0)
            def _():
                act(send(block, piece, width, 2, across))

        by_width(block, routes)

        @pl.when((core == 0) & (block >= 4))
        def _():
            act(send_low(block, piece))

    def pass_on(step, piece):
        zb, flip, block = block_at(step)

        @pl.when((step == 0) & (piece == 0))
        def _():
            own_copy.wait()

        @pl.when(step > 0)
        def _():
            by_width(block, lambda width: send(block, piece, width, 0, across).wait_recv())

        each_send(step, piece, lambda copy: copy.start())

        @pl.when(piece == PARTS - 1)
        def _():
            by_width(block, lambda width: keep(block, width).start())

    def multiply(step, piece):
        zb, flip, block = block_at(step)
        depth = block - 4 * core

        def squares(width):
            values = r_buf[block, pl.ds(piece * part, part), :width].astype(jnp.float32)
            var_out[:, :width] += jnp.sum(values * values, axis=0, keepdims=True)

        by_width(block, squares)
        for k in range(4):
            @pl.when(depth == k)
            def _(k=k):
                width = widths[k]

                @pl.when(piece == 0)
                def _():
                    r_masked[:, :width] = r_buf[block, :, :width] * mask_ref[0:1, :width].astype(jnp.bfloat16)

                @pl.when((piece == 0) & (core == 1))
                def _():
                    for each in range(PARTS):
                        send_low(4 + k, each).wait_recv()
                    low_masked[...] = r_low[k] * mask_ref[1:2, :].astype(jnp.bfloat16)

                @pl.when(core == 0)
                def _():
                    @pl.loop(0, span // CHUNK)
                    def _(j):
                        at = pl.ds(pl.multiple_of(piece * span + j * CHUNK, CHUNK), CHUNK)
                        p_buf[k, :, at] = jnp.dot(
                            r_masked[:, :width], x_own[:width, at], preferred_element_type=jnp.float32
                        ).astype(jnp.bfloat16)

                @pl.when(core == 1)
                def _():
                    @pl.loop(0, span // CHUNK)
                    def _(j):
                        at = pl.ds(pl.multiple_of(piece * span + j * CHUNK, CHUNK), CHUNK)
                        p_buf[k, :, at] = (
                            jnp.dot(low_masked[...], x_low[:, at], preferred_element_type=jnp.float32)
                            + jnp.dot(r_masked[:, :width], x_own[:width, at], preferred_element_type=jnp.float32)
                        ).astype(jnp.bfloat16)

                    send_p(4 + k, k, piece).start()

                keep_p(4 * core + k, k, piece).start()

    child_copy(0).start()

    @pl.when(core == 0)
    def _():
        send_x.start()

    var_out[...] = jnp.zeros_like(var_out)
    child_sum[...] = jnp.zeros_like(child_sum)
    first_low = 2 * (2 - z) * (1 - z // 2)

    def turn(n, carry):
        step, piece = n // PARTS, n % PARTS

        @pl.when(n < 8 * PARTS)
        def _():
            pass_on(step, piece)
            child_squares(n)

        @pl.when(n == LAG)
        def _():
            x_copy.wait()

        @pl.when((core == 1) & (n == first_low * PARTS + LAG))
        def _():
            send_x.wait_recv()

        @pl.when(n >= LAG)
        def _():
            multiply((n - LAG) // PARTS, (n - LAG) % PARTS)

        return carry

    lax.fori_loop(0, 8 * PARTS + LAG, turn, 0)
    child_out[...] = jnp.sum(child_sum[...], axis=0, keepdims=True)

    def finish(n, carry):
        each_send(n // PARTS, n % PARTS, lambda copy: copy.wait_send())
        return carry

    lax.fori_loop(0, 8 * PARTS, finish, 0)

    def kept(step, carry):
        block = block_at(step)[2]
        by_width(block, lambda width: keep(block, width).wait())
        return carry

    lax.fori_loop(0, 8, kept, 0)

    def product_done(n, carry):
        slot, piece = n // PARTS, n % PARTS
        keep_p(4 * core + slot, slot, piece).wait()

        @pl.when(core == 0)
        def _():
            send_p(4 + slot, slot, piece).wait_recv()

        @pl.when(core == 1)
        def _():
            send_p(4 + slot, slot, piece).wait_send()

        return carry

    lax.fori_loop(0, 4 * PARTS, product_done, 0)

    @pl.when(core == 0)
    def _():
        send_x.wait_send()


def gather_product(root_inv, child_off, child_inv, masks):
    rows, half = root_inv.shape
    cols = child_off.shape[1]
    bf16 = jnp.bfloat16
    dma = pltpu.SemaphoreType.DMA
    return pl.pallas_call(
        gather_kernel,
        out_shape=(
            jax.ShapeDtypeStruct((8 * rows, half), bf16),
            jax.ShapeDtypeStruct((8 * rows, cols), bf16),
            jax.ShapeDtypeStruct((1, half), jnp.float32),
            jax.ShapeDtypeStruct((1, cols), jnp.float32),
        ),
        in_specs=[
            pl.BlockSpec(memory_space=pl.ANY),
            pl.BlockSpec(memory_space=pl.ANY),
            pl.BlockSpec(memory_space=pl.ANY),
            pl.BlockSpec(memory_space=pltpu.VMEM),
        ],
        out_specs=(
            pl.BlockSpec(memory_space=pl.ANY),
            pl.BlockSpec(memory_space=pl.ANY),
            pl.BlockSpec(memory_space=pltpu.VMEM),
            pl.BlockSpec(memory_space=pltpu.VMEM),
        ),
        scratch_shapes=[
            pltpu.VMEM((8, rows, half), bf16),
            pltpu.VMEM((4, rows, half), bf16),
            pltpu.VMEM((half, cols), bf16),
            pltpu.VMEM((half, cols), bf16),
            pltpu.VMEM((4, rows, cols), bf16),
            pltpu.VMEM((rows, half), bf16),
            pltpu.VMEM((rows, half), bf16),
            pltpu.VMEM((2, child_inv.shape[0] // (8 * PARTS), cols), bf16),
            pltpu.VMEM((8, cols), jnp.float32),
            dma((8 * PARTS,)), dma((8 * PARTS, 4)), dma((4 * PARTS,)), dma((2,)), dma(()),
            dma((4 * PARTS,)), dma((4 * PARTS,)), dma((4 * PARTS,)), dma((8,)), dma(()), dma((2,)),
        ],
        compiler_params=pltpu.CompilerParams(
            collective_id=0, has_side_effects=True, vmem_limit_bytes=58 * 1024 * 1024
        ),
        cost_estimate=pl.CostEstimate(flops=36 * rows * rows * cols, bytes_accessed=60 * 2**20, transcendentals=0),
        name="gather_product",
    )(root_inv, child_off, child_inv, masks)


def cross_kernel(starts, flags_ref, r_ref, p_ref, off_ref, y_ref, var_ref, turned):
    @pl.when(pl.program_id(0) == 0)
    def _():
        for t in range(len(starts)):
            @pl.when(flags_ref[t] == 1)
            def _(t=t):
                turned[t * TILE : (t + 1) * TILE, :] = r_ref[:, t * TILE : (t + 1) * TILE].T

    var_ref[...] = jnp.zeros_like(var_ref)
    total = p_ref.shape[0]
    for t in range(len(starts)):
        tile = slice(t * TILE, (t + 1) * TILE)
        for core in range(2):
            @pl.when((flags_ref[t] == 1) & (flags_ref[len(starts)] == core))
            def _(t=t, core=core, tile=tile):
                low = core * (total // 2) + starts[t]
                y = -jnp.dot(turned[tile, low:], p_ref[low:, :], preferred_element_type=jnp.float32)
                y_ref[tile, :] = y
                var_ref[...] += jnp.sum(off_ref[tile, :].astype(jnp.float32) * y, axis=0, keepdims=True)

        @pl.when(flags_ref[t] == 0)
        def _(tile=tile):
            y_ref[tile, :] = jnp.zeros((TILE, y_ref.shape[1]), jnp.float32)


def cross_terms(flags, root_rows, product, child_off, rows):
    total, half = root_rows.shape
    cols = product.shape[1]
    widths = [min(half, -(-(k + 1) * rows // TILE) * TILE) for k in range(4)]
    starts = [rows * next(k for k in range(4) if widths[k] > t * TILE) for t in range(half // TILE)]
    return pl.pallas_call(
        functools.partial(cross_kernel, starts),
        grid_spec=pltpu.PrefetchScalarGridSpec(
            num_scalar_prefetch=1,
            grid=(cols // BLOCK,),
            in_specs=[
                pl.BlockSpec((total, half), lambda j, flags: (0, 0), pipeline_mode=pl.Buffered(1)),
                pl.BlockSpec((total, BLOCK), lambda j, flags: (0, j)),
                pl.BlockSpec((half, BLOCK), lambda j, flags: (0, j)),
            ],
            out_specs=[
                pl.BlockSpec((half, BLOCK), lambda j, flags: (0, j)),
                pl.BlockSpec((1, BLOCK), lambda j, flags: (0, j)),
            ],
            scratch_shapes=[pltpu.VMEM((half, total), jnp.bfloat16)],
        ),
        out_shape=(
            jax.ShapeDtypeStruct((half, cols), jnp.float32),
            jax.ShapeDtypeStruct((1, cols), jnp.float32),
        ),
        compiler_params=pltpu.CompilerParams(vmem_limit_bytes=56 * 1024 * 1024),
        name="cross_terms",
    )(flags, root_rows, product, child_off)


def fused_body(root_inv, child_off, child_inv, struct):
    rows, half = root_inv.shape
    cols = child_off.shape[1]
    tiles = half // TILE
    core = lax.axis_index("col")
    listed = lax.dynamic_slice_in_dim(struct, lax.axis_index("row") * cols // W1, 1, axis=0)[0]
    hits = jnp.any(jnp.arange(2 * tiles, dtype=jnp.int32)[:, None] == listed[None, :], axis=1)
    own_hits = lax.dynamic_slice_in_dim(hits, core * tiles, tiles, axis=0)
    masks = jnp.repeat(jnp.stack([own_hits, hits[:tiles]]).astype(jnp.float32), TILE, axis=1)
    root_rows, product, root_var, child_squares = gather_product(root_inv, child_off, child_inv, masks)
    flags = jnp.concatenate([own_hits.astype(jnp.int32), core[None].astype(jnp.int32)])
    cross_cov, cross_var = cross_terms(flags, root_rows, product, child_off, rows)
    local_terms = child_squares[0] - cross_var[0]
    return (cross_cov, root_var[0], lax.psum(local_terms, "col"))


def body(row_devices, col_devices, root_inv, child_off, child_inv, struct):
    rows, half = root_inv.shape
    cols = child_off.shape[1]
    fits = (
        row_devices == 8 and col_devices == 2 and half == 4 * rows and half % TILE == 0
        and rows % 64 == 0 and child_inv.shape[0] % 512 == 0 and half <= 1280 and cols <= 4096 and W1 % cols == 0 and cols % (PARTS * CHUNK) == 0 and cols % BLOCK == 0
    )
    run = fused_body if fits else plain_body
    return run(root_inv, child_off, child_inv, struct)


def solution(mesh):
    placed = (
        P(("cfg", "row"), "col"),
        P("col", ("cfg", "row")),
        P("col", ("cfg", "row")),
        P("cfg", None),
    )
    return jax.shard_map(
        functools.partial(body, mesh.shape["row"], mesh.shape["col"]),
        mesh=mesh,
        in_specs=placed,
        out_specs=(P("col", ("cfg", "row")), P(("cfg", "col")), P(("cfg", "row"))),
        check_vma=False,
    )
```
